32 devices in a mesh: groups: 2 (over y), gx: 4 (over z), gy: 2 (over x), gz: 2 (over core).
Axes of the slice: x: 2, y: 2, z: 4, core: 2. Of those that a mesh axis runs over, the one named last changes fastest.
Arguments:
- inputs: bfloat16 [1024, 6144], P(('groups', 'gx', 'gz'), 'gy'), parts along dimension 0, may hold values from -6 to 6
- cotangent: bfloat16 [1024, 6144], P(('groups', 'gx', 'gz'), 'gy'), parts along dimension 0, may hold values from -1.5 to 1.5
- up_weight: bfloat16 [49152, 6144], P(('gx', 'gz'), 'gy'), may hold values from -0.078125 to 0.078125
- down_weight: bfloat16 [49152, 6144], P(('gx', 'gz'), 'gy'), may hold values from -0.02734375 to 0.02734375
Outputs:
- outputs: bfloat16 [1024, 6144], P(('groups', 'gx', 'gz'), 'gy'), parts along dimension 0
- input_grad: bfloat16 [1024, 6144], P(('groups', 'gx', 'gz'), 'gy'), parts along dimension 0
The draws below stay inside these ranges and needn't reach their ends.
There are 2 independent parts, one for each index of `groups`. The reference program is written for one: setup_inputs(seed, part) draws one part's arguments, and reference() takes and returns one part's arrays. A program takes and returns all parts, laid end to end along the dimension named above; an argument that names none is the same for every part. Nothing has to cross between parts.
All inputs are finite; a program needn't handle non-finite values.
Results may differ from the reference program's by a relative error of at most 0.018.
Values may be sent and summed in bfloat16 or wider, within the bound.
A program may use at most 256 MiB of HBM per device.

```python
import jax
import jax.numpy as jnp
from jax import lax

D = 6144
FF = 49152
TOKENS = 512
N_GX = 4
N_GY = 2
N_GZ = 2


def level_of(key, shape, cuts, least, high):
    factor_of = 1.0
    for position, shards_of in cuts:
        draws = jax.random.uniform(jax.random.fold_in(jax.random.fold_in(key, 6), position), (shards_of,), jnp.float32, least / len(cuts), high / len(cuts))
        factor_of = factor_of * jnp.repeat(jnp.exp(draws), shape[position] // shards_of).reshape((-1,) + (1,) * (len(shape) - 1 - position))
    return factor_of


def scatter_about(stream_key, extent, scale, reach, cuts=(), held_as=jnp.bfloat16):
    array = jax.random.normal(stream_key, extent, jnp.float32) * scale
    if len(cuts) > 0:
        array = level_of(stream_key, extent, cuts, -0.22, 0.18) * array
    return jnp.clip(array, min=-reach, max=reach).astype(held_as)


def setup_inputs(seed: int = 0, part: int = 0) -> dict:
    seeds = jax.random.split(jax.random.key(seed), 5)
    own_keys = jax.random.split(jax.random.fold_in(seeds[4], part), 5)
    inputs = scatter_about(own_keys[0], (TOKENS, D), 1.0, 6.0, ((0, 8), (1, 2)))
    cotangent = scatter_about(own_keys[1], (TOKENS, D), 0.25, 1.5, ((0, 8), (1, 2)))
    up_weight = scatter_about(seeds[2], (FF, D), D ** -0.5, 0.078125, ((0, 8), (1, 2)))
    down_weight = scatter_about(seeds[3], (FF, D), FF ** -0.5, 0.02734375, ((0, 8), (1, 2)))
    return {"inputs": inputs, "cotangent": cotangent, "up_weight": up_weight, "down_weight": down_weight}


gelu_const = 0.7978845608028654


def gelu_value(value):
    inner = gelu_const * (value + 0.044715 * value * value * value)
    return 0.5 * value * (1.0 + jnp.tanh(inner))


def gelu_slope(value):
    inner = gelu_const * (value + 0.044715 * value * value * value)
    tanh_val = jnp.tanh(inner)
    return 0.5 * (1.0 + tanh_val) + 0.5 * value * (1.0 - tanh_val * tanh_val) * gelu_const * (1.0 + 3.0 * 0.044715 * value * value)


def rounded(term):
    return lax.optimization_barrier(term.astype(jnp.bfloat16)).astype(jnp.float32)


def sum_inner(left, right, blocks):
    width = left.shape[1] // blocks

    def step(total, index):
        start = (index * width).astype(jnp.int32)
        part_left = lax.dynamic_slice_in_dim(left, start, width, 1)
        part_right = lax.dynamic_slice_in_dim(right, start, width, 1)
        term = lax.dot_general(part_left, part_right, (((1,), (1,)), ((), ())), preferred_element_type=jnp.float32)
        return total + rounded(term), None

    init = jnp.zeros((left.shape[0], right.shape[0]), jnp.float32)
    total, unused = lax.scan(step, init, jnp.arange(blocks, dtype=jnp.int32))
    return total


def sum_outer(left, right, blocks):
    width = left.shape[1] // blocks

    def step(total, index):
        start = (index * width).astype(jnp.int32)
        part_left = lax.dynamic_slice_in_dim(left, start, width, 1)
        part_right = lax.dynamic_slice_in_dim(right, start, width, 0)
        term = jnp.dot(part_left, part_right, preferred_element_type=jnp.float32)
        return total + rounded(term), None

    init = jnp.zeros((left.shape[0], right.shape[1]), jnp.float32)
    total, unused = lax.scan(step, init, jnp.arange(blocks, dtype=jnp.int32))
    return total


def reference(inputs, cotangent, up_weight, down_weight):
    hidden = sum_inner(inputs, up_weight, N_GY)
    act = gelu_value(hidden).astype(jnp.bfloat16)
    outputs = sum_outer(act, down_weight, N_GX * N_GZ).astype(jnp.bfloat16)
    slope = sum_inner(cotangent, down_weight, N_GY)
    hidden_grad = (slope * gelu_slope(hidden)).astype(jnp.bfloat16)
    input_grad = sum_outer(hidden_grad, up_weight, N_GX * N_GZ).astype(jnp.bfloat16)
    return (outputs, input_grad)
```

```python
import jax
import jax.numpy as jnp
from jax import lax
from jax.sharding import PartitionSpec as P

gelu_const = 0.7978845608028654


def gelu_value(value):
    inner = gelu_const * (value + 0.044715 * value * value * value)
    return 0.5 * value * (1.0 + jnp.tanh(inner))


def gelu_slope(value):
    inner = gelu_const * (value + 0.044715 * value * value * value)
    tanh_val = jnp.tanh(inner)
    return 0.5 * (1.0 + tanh_val) + 0.5 * value * (1.0 - tanh_val * tanh_val) * gelu_const * (
        1.0 + 3.0 * 0.044715 * value * value
    )


def inner_product(left, right):
    return lax.dot_general(
        left, right, (((1,), (1,)), ((), ())), preferred_element_type=jnp.float32
    )


def inner_term(left, right):
    return inner_product(left, right)


def outer_term(left, right):
    return jnp.dot(left, right, preferred_element_type=jnp.float32)


def body(inputs, cotangent, up_weight, down_weight):
    seen_inputs, seen_cotangent = (
        lax.all_gather(inputs, ("gx", "gz"), axis=0, tiled=True),
        lax.all_gather(cotangent, ("gx", "gz"), axis=0, tiled=True),
    )
    hidden_share = lax.psum_scatter(
        inner_term(seen_inputs, up_weight).astype(jnp.bfloat16),
        "gy",
        scatter_dimension=0,
        tiled=True,
    ).astype(jnp.float32)
    act_share = gelu_value(hidden_share).astype(jnp.bfloat16)
    act_rows = lax.all_gather(act_share, "gy", axis=0, tiled=True)
    outputs = lax.psum_scatter(
        outer_term(act_rows, down_weight).astype(jnp.bfloat16),
        ("gx", "gz"),
        scatter_dimension=0,
        tiled=True,
    )
    slope_share = lax.psum_scatter(
        inner_term(seen_cotangent, down_weight).astype(jnp.bfloat16),
        "gy",
        scatter_dimension=0,
        tiled=True,
    ).astype(jnp.float32)
    grad_share = (slope_share * gelu_slope(hidden_share)).astype(jnp.bfloat16)
    grad_rows = lax.all_gather(grad_share, "gy", axis=0, tiled=True)
    input_grad = lax.psum_scatter(
        outer_term(grad_rows, up_weight).astype(jnp.bfloat16),
        ("gx", "gz"),
        scatter_dimension=0,
        tiled=True,
    )
    return (outputs, input_grad)


def ordered(value, earlier):
    return lax.optimization_barrier((value, earlier))[0]


def pair_body(pieces, inputs, cotangent, up_weight, down_weight):
    width = up_weight.shape[0] // pieces
    sent = []

    def swap(term):
        if len(sent) >= 2:
            term = ordered(term, sent[-2])
        other = lax.ppermute(term, "gy", [(0, 1), (1, 0)])
        sent.append(other)
        return other

    def gather(rows):
        return lax.all_gather(rows, ("gx", "gz"), axis=0, tiled=True)

    def scatter(total):
        return lax.psum_scatter(
            total.astype(jnp.bfloat16), ("gx", "gz"), scatter_dimension=0, tiled=True
        )

    def part(weight, piece):
        return weight[piece * width : (piece + 1) * width]

    seen_inputs = gather(inputs)
    seen_cotangent = gather(ordered(cotangent, inputs))
    hidden = []
    for piece in range(pieces):
        term = inner_term(seen_inputs, part(up_weight, piece)).astype(jnp.bfloat16)
        hidden.append((term, swap(term)))
    slope = []
    for piece in range(pieces):
        term = inner_term(seen_cotangent, part(down_weight, piece)).astype(jnp.bfloat16)
        slope.append((term, swap(term)))
    values = [a.astype(jnp.float32) + b.astype(jnp.float32) for a, b in hidden]
    out_total = 0.0
    for piece in range(pieces):
        act = gelu_value(values[piece]).astype(jnp.bfloat16)
        out_total += outer_term(act, part(down_weight, piece))
    outputs = scatter(out_total)
    grad_total = 0.0
    for piece in range(pieces):
        a, b = slope[piece]
        total = a.astype(jnp.float32) + b.astype(jnp.float32)
        grad = (total * gelu_slope(values[piece])).astype(jnp.bfloat16)
        grad_total += outer_term(grad, part(up_weight, piece))
    return (outputs, scatter(grad_total))


def chosen_body(mesh):
    def run(inputs, cotangent, up_weight, down_weight):
        if mesh.shape["gy"] != 2 or up_weight.shape[0] % 1024 != 0:
            return body(inputs, cotangent, up_weight, down_weight)
        return pair_body(4, inputs, cotangent, up_weight, down_weight)

    return run


def solution(mesh):
    placed = (
        P(("groups", "gx", "gz"), "gy"),
        P(("groups", "gx", "gz"), "gy"),
        P(("gx", "gz"), "gy"),
        P(("gx", "gz"), "gy"),
    )
    return jax.shard_map(
        chosen_body(mesh),
        mesh=mesh,
        in_specs=placed,
        out_specs=(P(("groups", "gx", "gz"), "gy"), P(("groups", "gx", "gz"), "gy")),
        check_vma=False,
    )
```

```python
import jax
import jax.numpy as jnp
from jax import lax
from jax.experimental import pallas as pl
from jax.experimental.pallas import tpu as pltpu
from jax.sharding import PartitionSpec as P

gelu_const = 0.7978845608028654


def gelu_value(value):
    inner = gelu_const * (value + 0.044715 * value * value * value)
    return 0.5 * value * (1.0 + jnp.tanh(inner))


def gelu_slope(value):
    inner = gelu_const * (value + 0.044715 * value * value * value)
    tanh_val = jnp.tanh(inner)
    return 0.5 * (1.0 + tanh_val) + 0.5 * value * (1.0 - tanh_val * tanh_val) * gelu_const * (
        1.0 + 3.0 * 0.044715 * value * value
    )


def inner_product(left, right):
    return lax.dot_general(
        left, right, (((1,), (1,)), ((), ())), preferred_element_type=jnp.float32
    )


def inner_term(left, right):
    return inner_product(left, right)


def outer_term(left, right):
    return jnp.dot(left, right, preferred_element_type=jnp.float32)


def body(inputs, cotangent, up_weight, down_weight):
    seen_inputs, seen_cotangent = (
        lax.all_gather(inputs, ("gx", "gz"), axis=0, tiled=True),
        lax.all_gather(cotangent, ("gx", "gz"), axis=0, tiled=True),
    )
    hidden_share = lax.psum_scatter(
        inner_term(seen_inputs, up_weight).astype(jnp.bfloat16),
        "gy",
        scatter_dimension=0,
        tiled=True,
    ).astype(jnp.float32)
    act_share = gelu_value(hidden_share).astype(jnp.bfloat16)
    act_rows = lax.all_gather(act_share, "gy", axis=0, tiled=True)
    outputs = lax.psum_scatter(
        outer_term(act_rows, down_weight).astype(jnp.bfloat16),
        ("gx", "gz"),
        scatter_dimension=0,
        tiled=True,
    )
    slope_share = lax.psum_scatter(
        inner_term(seen_cotangent, down_weight).astype(jnp.bfloat16),
        "gy",
        scatter_dimension=0,
        tiled=True,
    ).astype(jnp.float32)
    grad_share = (slope_share * gelu_slope(hidden_share)).astype(jnp.bfloat16)
    grad_rows = lax.all_gather(grad_share, "gy", axis=0, tiled=True)
    input_grad = lax.psum_scatter(
        outer_term(grad_rows, up_weight).astype(jnp.bfloat16),
        ("gx", "gz"),
        scatter_dimension=0,
        tiled=True,
    )
    return (outputs, input_grad)


def ordered(value, earlier):
    return lax.optimization_barrier((value, earlier))[0]


vmem_bytes = 48 * 1024 * 1024
light = pl.CostEstimate(flops=1, bytes_accessed=1, transcendentals=0)


def inner_kernel(seen_ref, weight_ref, out_ref):
    made = inner_product(seen_ref[...], weight_ref[...])
    out_ref[...] = made.astype(out_ref.dtype)


def inner_call(seen, weight, piece, pieces):
    tokens, depth = seen.shape
    width = weight.shape[0] // pieces
    tile = 256
    blocks = width // tile
    return pl.pallas_call(
        inner_kernel,
        grid=(blocks,),
        out_shape=jax.ShapeDtypeStruct((tokens, width), jnp.bfloat16),
        in_specs=[
            pl.BlockSpec((tokens, depth), lambda i: (0, 0)),
            pl.BlockSpec((tile, depth), lambda i: (piece * blocks + i, 0)),
        ],
        out_specs=pl.BlockSpec((tokens, tile), lambda i: (0, i)),
        compiler_params=pltpu.CompilerParams(vmem_limit_bytes=vmem_bytes),
        cost_estimate=light,
    )(seen, weight)


def outer_kernel(pairs, resumed, *refs):
    shares, rest = refs[: 2 * pairs], refs[2 * pairs :]
    weight_ref, out_ref = rest[0], rest[-1]

    @pl.when(pl.program_id(0) == 0)
    def begin():
        out_ref[...] = rest[1][...] if resumed else jnp.zeros_like(out_ref)

    sums = [
        shares[2 * i][...].astype(jnp.float32) + shares[2 * i + 1][...].astype(jnp.float32)
        for i in range(pairs)
    ]
    if pairs == 1:
        share = gelu_value(sums[0])
    else:
        share = sums[0] * gelu_slope(sums[1])
    out_ref[...] += outer_term(share.astype(jnp.bfloat16), weight_ref[...])


def outer_call(total, shares, weight, piece):
    tokens, width = shares[0].shape
    columns = weight.shape[1]
    tile = 512
    blocks = width // tile
    whole = pl.BlockSpec((tokens, columns), lambda i: (0, 0))
    resumed = total is not None
    return pl.pallas_call(
        lambda *refs: outer_kernel(len(shares) // 2, resumed, *refs),
        grid=(blocks,),
        out_shape=jax.ShapeDtypeStruct((tokens, columns), jnp.float32),
        in_specs=[pl.BlockSpec((tokens, tile), lambda i: (0, i))] * len(shares)
        + [pl.BlockSpec((tile, columns), lambda i: (piece * blocks + i, 0))]
        + [whole] * resumed,
        out_specs=whole,
        compiler_params=pltpu.CompilerParams(vmem_limit_bytes=vmem_bytes),
        cost_estimate=light,
    )(*shares, weight, *([total] * resumed))


def place_kernel(chips, rows, chip_ref, total_ref, out_ref):
    chip = chip_ref[0]
    for step in range(chips):
        start = pl.multiple_of(lax.rem(chip + step, chips) * rows, rows)
        if step == 0:
            block = jnp.zeros((rows, out_ref.shape[1]), out_ref.dtype)
        else:
            block = total_ref[(step - 1) * rows : step * rows, :].astype(out_ref.dtype)
        out_ref[pl.ds(start, rows), :] = block


def place_call(total, chip, chips, rows):
    columns = total.shape[1]
    tile = columns // 4
    return pl.pallas_call(
        lambda *refs: place_kernel(chips, rows, *refs),
        grid=(4,),
        out_shape=jax.ShapeDtypeStruct((chips * rows, columns), jnp.bfloat16),
        in_specs=[
            pl.BlockSpec(memory_space=pltpu.SMEM),
            pl.BlockSpec((total.shape[0], tile), lambda i: (0, i)),
        ],
        out_specs=pl.BlockSpec((chips * rows, tile), lambda i: (0, i)),
        compiler_params=pltpu.CompilerParams(vmem_limit_bytes=vmem_bytes),
        cost_estimate=light,
    )(jnp.reshape(chip, (1,)).astype(jnp.int32), total)


swapped = [(0, 1), (1, 0)]


def pair_body(chips, near_cut, far_cut, inputs, cotangent, up_weight, down_weight):
    units = up_weight.shape[0]
    rows = 2 * inputs.shape[0]
    chip = lax.axis_index("gx")
    others = [lax.rem(chip + step, chips) * rows for step in range(1, chips)]
    sent = []

    def swap(term):
        if len(sent) >= 2:
            term = ordered(term, sent[-2])
        other = lax.ppermute(term, "gy", swapped)
        sent.append(other)
        return (term, other)

    def near_rows(mine):
        return jnp.concatenate([mine, lax.ppermute(mine, "gz", swapped)])

    def far_rows(mine):
        seen = lax.all_gather(mine, ("gx", "gz"), axis=0, tiled=True)
        return jnp.concatenate(
            [lax.dynamic_slice_in_dim(seen, start, rows, 0) for start in others]
        )

    last = [inputs]

    def after(values, *earlier):
        return lax.optimization_barrier((values, last[0]) + earlier)[0]

    def scatter(total, *earlier):
        placed = place_call(after(total, *earlier), chip, chips, rows)
        last[0] = placed
        return lax.psum_scatter(placed, ("gx", "gz"), scatter_dimension=0, tiled=True)

    def term(seen, weight, piece, pieces, *earlier):
        seen = after(seen, *earlier)
        made = inner_call(seen, weight, piece, pieces)
        last[0] = made
        return made

    def add_act(total, hidden, piece):
        last[0] = outer_call(total, after(hidden[piece]), down_weight, piece)
        return last[0]

    def add_grad(total, slope, hidden, piece):
        shares = after(slope[piece] + hidden[piece])
        last[0] = outer_call(total, shares, up_weight, piece)
        return last[0]

    def finish(far, near):
        near = near.astype(jnp.bfloat16)
        half = rows // 2
        other = lax.ppermute(near[half:], "gz", swapped)
        total = far.astype(jnp.float32) + near[:half].astype(jnp.float32)
        return (total + other.astype(jnp.float32)).astype(jnp.bfloat16)

    near_inputs = near_rows(inputs)
    far_inputs = far_rows(inputs)
    near_cotangent = near_rows(ordered(cotangent, near_inputs))
    far_cotangent = far_rows(ordered(cotangent, inputs))

    near_hidden = [
        swap(term(near_inputs, up_weight, piece, near_cut)) for piece in range(near_cut)
    ]
    near_terms = []

    def near_term():
        index = len(near_terms)
        near_terms.append(term(near_cotangent, down_weight, index, near_cut))

    near_term()
    far_hidden, far_slope, near_slope = [], [], []
    near_out, near_grad, far_out, far_grad = None, None, None, None
    for piece in range(far_cut):
        made = term(far_inputs, up_weight, piece, far_cut, sent[-2])
        far_hidden.append(swap(made))
        if piece == 1:
            for index in range(near_cut):
                near_out = add_act(near_out, near_hidden, index)
            near_term()
        if piece >= 2:
            far_out = add_act(far_out, far_hidden, piece - 2)
    for piece in range(far_cut):
        if piece == 3:
            far_outputs = scatter(far_out, sent[-2])
        made = term(far_cotangent, down_weight, piece, far_cut, sent[-2])
        far_slope.append(swap(made))
        if piece < 2:
            far_out = add_act(far_out, far_hidden, far_cut - 2 + piece)
            if piece == 1:
                near_term()
        else:
            far_grad = add_grad(far_grad, far_slope, far_hidden, piece - 2)
    for piece in range(near_cut):
        near_slope.append(swap(near_terms[piece]))
        if piece < 2:
            index = far_cut - 2 + piece
            far_grad = add_grad(far_grad, far_slope, far_hidden, index)
    far_gradient = scatter(far_grad)
    for piece in range(near_cut):
        near_grad = add_grad(near_grad, near_slope, near_hidden, piece)
    return (finish(far_outputs, near_out), finish(far_gradient, near_grad))


def chosen_body(mesh):
    def run(inputs, cotangent, up_weight, down_weight):
        sizes = mesh.shape
        if sizes["gy"] != 2 or sizes["gz"] != 2 or up_weight.shape[0] % 6144 != 0:
            return body(inputs, cotangent, up_weight, down_weight)
        return pair_body(sizes["gx"], 3, 4, inputs, cotangent, up_weight, down_weight)

    return run


def solution(mesh):
    placed = (
        P(("groups", "gx", "gz"), "gy"),
        P(("groups", "gx", "gz"), "gy"),
        P(("gx", "gz"), "gy"),
        P(("gx", "gz"), "gy"),
    )
    return jax.shard_map(
        chosen_body(mesh),
        mesh=mesh,
        in_specs=placed,
        out_specs=(P(("groups", "gx", "gz"), "gy"), P(("groups", "gx", "gz"), "gy")),
        check_vma=False,
    )
```
